256 devices in a mesh: grp: 32 (over z_lo, y, core), tp: 8 (over x, z_hi).
Axes of the slice: x: 4, y: 4, z: 8 (z_hi: 2, z_lo: 4; z = z_hi * 4 + z_lo), core: 2. Of those that a mesh axis runs over, the one named last changes fastest.
Arguments:
- latents: bfloat16 [32768, 2048], P('grp', 'tp'), may hold values from -6 to 6
- parents: bfloat16 [128, 16, 2048], P('grp'), may hold values from -6 to 6
- parent_pairs: int32 [128, 2], P('grp'), may hold values from 0 to 127, as said below
- timestep: int32 [128], P('grp'), may hold values from 0 to 999
- valid_frames: int32 [128], P('grp'), may hold values from 4 to 16, as said below
- w_mod: bfloat16 [256, 6, 2048], P(None, None, 'tp'), may hold values from -0.375 to 0.375
- w_qkv: bfloat16 [2048, 3, 16, 128], P(None, None, 'tp'), may hold values from -0.125 to 0.125
- w_out: bfloat16 [16, 128, 2048], P('tp'), may hold values from -0.1875 to 0.1875
- w_cq: bfloat16 [2048, 16, 128], P(None, 'tp'), may hold values from -0.125 to 0.125
- w_ckv: bfloat16 [2048, 2, 16, 128], P(None, None, 'tp'), may hold values from -0.125 to 0.125
- w_cout: bfloat16 [16, 128, 2048], P('tp'), may hold values from -0.1875 to 0.1875
Outputs:
- next_frames: bfloat16 [32, 64, 16, 2048], P(None, 'grp', None, 'tp')
The draws below stay inside these ranges and needn't reach their ends.
Inputs may be any that keep to these rules, and one draw needn't show every extreme that they name: `parent_pairs`: the first parent of group g is g - 1 or g, the second is g or g + 1, both kept within 0 to 127. Where g is a multiple of 4, the first parent is g - 1 (for g > 0); where g + 1 is a multiple of 4, the second is g + 1 (for g < 127). `valid_frames`: frames of a group at or past its count are padding and are never attended to.
All inputs are finite; a program needn't handle non-finite values.
Results may differ from the reference program's by a relative error of at most 0.019.
Values may be sent and summed in bfloat16 or wider, within the bound.
A program may use at most 128 MiB of HBM per device.

```python
import math
import jax
import jax.numpy as jnp
from jax import lax

D = 2048
H = 16
HD = 128
TEMB = 256
F = 16
P_SIZE = 16
GDEV = 4
G = 128
TOK = 32768
N_GRP = 32


def draw_parent_pairs(key, part):
    key = jax.random.fold_in(key, 11)
    first_key, second_key = jax.random.split(key)
    index = jnp.arange(G, dtype=jnp.int32)
    place = index % GDEV
    first_step = jnp.where(place == 0, 1, jax.random.randint(first_key, (G,), 0, 2))
    second_step = jnp.where(place == GDEV - 1, 1, jax.random.randint(second_key, (G,), 0, 2))
    first = jnp.clip(index - first_step, 0, G - 1)
    second = jnp.clip(index + second_step, 0, G - 1)
    return jnp.stack([first, second], axis=1).astype(jnp.int32)


def draw_valid_frames(key, part):
    key = jax.random.fold_in(key, 23)
    count_key, place_key = jax.random.split(key)
    counts = jax.random.randint(count_key, (G,), 4, F + 1)
    where = jax.random.randint(place_key, (), 0, G)
    counts = counts.at[where].set(F)
    counts = counts.at[(where + 1) % G].set(4)
    return counts.astype(jnp.int32)


def plant(drawn, own_key, low, top_value):
    longest = drawn.shape.index(max(drawn.shape))
    spots = []
    for shift in (0, 1):
        where = [jax.random.randint(jax.random.fold_in(own_key, axis), (), 0, length) for axis, length in enumerate(drawn.shape)]
        where[longest] = (where[longest] + shift) % drawn.shape[longest]
        spots.append(tuple(where))
    return drawn.at[spots[0]].set(low).at[spots[1]].set(top_value)


def with_spikes(values, key, source, target, blocks, factor):
    owner, partner = [(jnp.arange(values.shape[axis_at]) // (values.shape[axis_at] // blocks)).reshape([-1 if axis == axis_at else 1 for axis in range(values.ndim)]) for axis_at in (source, target)]
    chosen = jax.random.permutation(key, blocks)[partner]
    strong = (owner == chosen) | (owner == (partner + blocks // 2) % blocks)
    return jnp.where(strong, factor * values, values)


def block_scale(rng, extent, shards, least, top_value):
    factor_of = 1.0
    for dim, shards_of in shards:
        steps = jax.random.uniform(jax.random.fold_in(jax.random.fold_in(rng, 6), dim), (shards_of,), jnp.float32, least / len(shards), top_value / len(shards))
        factor_of = factor_of * jnp.repeat(jnp.exp(steps), extent[dim] // shards_of).reshape((-1,) + (1,) * (len(extent) - 1 - dim))
    return factor_of


def normal_values(key, extent, scale, bound, cuts=(), kind=jnp.bfloat16):
    entries = jax.random.normal(key, extent, jnp.float32) * scale
    if len(cuts) > 0:
        entries = block_scale(key, extent, cuts, -0.22, 0.18) * entries
    return jnp.clip(entries, min=-bound, max=bound).astype(kind)


def heavy_noise(key, shape, deviation, bound, cuts, heavy, kind=jnp.bfloat16):
    values = deviation * jax.random.normal(key, shape, jnp.float32)
    if cuts:
        values = values * block_scale(key, shape, cuts, -0.22, 0.18)
    return jnp.clip(with_spikes(values, jax.random.fold_in(key, 3), *heavy), -bound, bound).astype(kind)


def setup_inputs(seed: int = 0) -> dict:
    seeds = jax.random.split(jax.random.key(seed), 12)
    latents = normal_values(seeds[0], (TOK, D), 1.0, 6.0, ((0, 32), (1, 8)))
    parents = normal_values(seeds[1], (G, P_SIZE, D), 1.0, 6.0, ((0, 32),))
    parent_pairs = draw_parent_pairs(jax.random.fold_in(seeds[11], 71), 0)
    timestep = plant(jax.random.randint(seeds[3], (G,), 0, 1000), jax.random.fold_in(seeds[3], 1), 0, 999).astype(jnp.int32)
    valid_frames = draw_valid_frames(jax.random.fold_in(seeds[11], 71), 0)
    w_mod = normal_values(seeds[5], (TEMB, 6, D), TEMB ** -0.5, 0.375, ((2, 8),))
    w_qkv = normal_values(seeds[6], (D, 3, H, HD), D ** -0.5, 0.125, ((2, 8),))
    w_out = heavy_noise(seeds[7], (H, HD, D), D ** -0.5, 0.1875, ((0, 8),), (0, 2, 8, 2.0))
    w_cq = normal_values(seeds[8], (D, H, HD), D ** -0.5, 0.125, ((1, 8),))
    w_ckv = normal_values(seeds[9], (D, 2, H, HD), D ** -0.5, 0.125, ((2, 8),))
    w_cout = heavy_noise(seeds[10], (H, HD, D), D ** -0.5, 0.1875, ((0, 8),), (0, 2, 8, 2.0))
    return dict(latents=latents, parents=parents, parent_pairs=parent_pairs, timestep=timestep, valid_frames=valid_frames, w_mod=w_mod, w_qkv=w_qkv, w_out=w_out, w_cq=w_cq, w_ckv=w_ckv, w_cout=w_cout)


def embed_time(stamp):
    half = TEMB // 2
    freq = jnp.exp(-math.log(10000.0) * jnp.arange(half, dtype=jnp.float32) / half)
    angle = stamp.astype(jnp.float32)[..., None] * freq
    return jax.nn.silu(jnp.concatenate([jnp.cos(angle), jnp.sin(angle)], axis=-1)).astype(jnp.bfloat16)

def layer_norm(values):
    centre = values - lax.optimization_barrier(jnp.mean(values, axis=-1, keepdims=True))
    spread = lax.optimization_barrier(jnp.mean(centre * centre, axis=-1, keepdims=True))
    return centre * lax.rsqrt(spread + 1e-06)

def attend(query, keys, vals, keep):
    scores = jnp.einsum('qhe,khe->hqk', query.astype(jnp.float32), keys.astype(jnp.float32)) / math.sqrt(HD)
    weights = jnp.exp(scores) * keep[None, None, :]
    probs = (weights / lax.optimization_barrier(jnp.sum(weights, axis=-1, keepdims=True))).astype(jnp.bfloat16)
    return jnp.einsum('hqk,khe->qhe', probs.astype(jnp.float32), vals.astype(jnp.float32)).astype(jnp.bfloat16)

def reference(latents, parents, parent_pairs, timestep, valid_frames, w_mod, w_qkv, w_out, w_cq, w_ckv, w_cout):
    rows = F * P_SIZE

    def one_group(items):
        tokens, stamp, valid, pair = items
        temb = embed_time(stamp[None])
        mod = jnp.dot(temb, w_mod.reshape(TEMB, 6 * D), preferred_element_type=jnp.float32)
        mod = mod.astype(jnp.bfloat16).astype(jnp.float32).reshape(6, D)
        hidden = (layer_norm(tokens.astype(jnp.float32)) * (1.0 + mod[1]) + mod[0]).astype(jnp.bfloat16)
        qkv = jnp.dot(hidden, w_qkv.reshape(D, 3 * H * HD), preferred_element_type=jnp.float32)
        qkv = qkv.astype(jnp.bfloat16).reshape(rows, 3, H, HD)
        frame = jnp.arange(rows, dtype=jnp.int32) // P_SIZE
        keep = (frame < valid).astype(jnp.float32)
        attn = attend(qkv[:, 0], qkv[:, 1], qkv[:, 2], keep).reshape(rows, H * HD)
        branch = jnp.dot(attn, w_out.reshape(H * HD, D), preferred_element_type=jnp.float32)
        x_one = (tokens.astype(jnp.float32) + mod[2] * branch).astype(jnp.bfloat16)
        hidden2 = (layer_norm(x_one.astype(jnp.float32)) * (1.0 + mod[4]) + mod[3]).astype(jnp.bfloat16)
        cross_q = jnp.dot(hidden2, w_cq.reshape(D, H * HD), preferred_element_type=jnp.float32)
        cross_q = cross_q.astype(jnp.bfloat16).reshape(rows, H, HD)
        chosen = jnp.take(parents, pair.astype(jnp.int32), axis=0).reshape(2 * P_SIZE, D)
        cross_kv = jnp.dot(chosen, w_ckv.reshape(D, 2 * H * HD), preferred_element_type=jnp.float32)
        cross_kv = cross_kv.astype(jnp.bfloat16).reshape(2 * P_SIZE, 2, H, HD)
        ones = jnp.ones((2 * P_SIZE,), jnp.float32)
        cattn = attend(cross_q, cross_kv[:, 0], cross_kv[:, 1], ones).reshape(rows, H * HD)
        branch2 = jnp.dot(cattn, w_cout.reshape(H * HD, D), preferred_element_type=jnp.float32)
        return (x_one.astype(jnp.float32) + mod[5] * branch2).astype(jnp.bfloat16)
    groups = parent_pairs.shape[0]
    result = lax.map(one_group, (latents.reshape(groups, rows, D), timestep, valid_frames, parent_pairs))
    return result.reshape(N_GRP, groups * F // N_GRP, P_SIZE, D)
```

```python
import math

import jax
import jax.numpy as jnp
from jax import lax
from jax.experimental import pallas as pl
from jax.experimental.pallas import tpu as pltpu
from jax.sharding import PartitionSpec as P

D = 2048
HD = 128
TEMB = 256
F = 16
P_SIZE = 16
ROWS = F * P_SIZE
EXT = ROWS + 16
MESH = pl.DeviceIdType.MESH
BF = jnp.bfloat16
F32 = jnp.float32
QUERY, CROSS, OUT, COUT = range(4)
WEIGHT_ROWS = (D, D, 2 * HD, 2 * HD)


def embed_time(stamp):
    half = TEMB // 2
    freq = jnp.exp(-math.log(10000.0) * jnp.arange(half, dtype=jnp.float32) / half)
    angle = stamp.astype(jnp.float32)[..., None] * freq
    return jax.nn.silu(jnp.concatenate([jnp.cos(angle), jnp.sin(angle)], axis=-1)).astype(BF)


def norm_rows(values, scale, shift):
    centre = values - jnp.mean(values, axis=-1, keepdims=True)
    spread = jnp.mean(centre * centre, axis=-1, keepdims=True)
    return centre * lax.rsqrt(spread + 1e-06) * (1.0 + scale) + shift


def kernel(
    lat, modx, parents, wqkv, wckv, wcq, wout, wcout, pairs, out,
    rows_all, z_source, w_query, w_cross, w_out, w_cout, table, chosen, hidden, qkv, attn,
    branch_send, branch_recv, fold_send, fold, x_one, result, blocks,
    local_sem, send_sem, recv_sem, final_sem, out_sem,
):
    grp, tp = lax.axis_index("grp"), lax.axis_index("tp")
    c, y, zlo = lax.rem(grp, 2), lax.rem(lax.div(grp, 2), 4), lax.div(grp, 8)
    x, zhi = lax.div(tp, 2), lax.rem(tp, 2)
    z = zhi * 4 + zlo
    other = 1 - zhi
    step_z = 1 - 2 * c
    place = c * 3 + step_z * zlo
    is_source = lax.div(place, 3)

    def dev(dx=0, dy=0, dz=0, dc=0):
        xx, yy = lax.rem(x + dx + 4, 4), lax.rem(y + dy + 4, 4)
        zz, cc = lax.rem(z + dz + 8, 8), lax.rem(c + dc, 2)
        return {
            "grp": (lax.rem(zz, 4) * 4 + yy) * 2 + cc,
            "tp": xx * 2 + lax.div(zz, 4),
        }

    names = {}

    def sem_id(*name):
        return names.setdefault(name, len(names))

    sends = []

    def remote(src, dst, name, target, extra=0, note=True):
        copy = pltpu.make_async_remote_copy(
            src_ref=src, dst_ref=dst, send_sem=send_sem.at[sem_id(*name)],
            recv_sem=recv_sem.at[sem_id(*name) + extra], device_id=target, device_id_type=MESH,
        )
        if note:
            sends.append(copy)
        return copy

    def arrived(region, name, extra=0):
        pltpu.make_async_remote_copy(
            src_ref=region, dst_ref=region, send_sem=send_sem.at[0],
            recv_sem=recv_sem.at[sem_id(*name) + extra], device_id=dev(dc=1), device_id_type=MESH,
        ).wait_recv()

    locals_used = [0]

    def local(src, dst):
        copy = pltpu.make_async_copy(src, dst, local_sem.at[locals_used[0]])
        locals_used[0] += 1
        copy.start()
        return copy

    def columns(index):
        return pl.ds(pl.multiple_of(index * 256, 256), 256)

    load_z = [
        local(lat.at[pl.ds(2 * other, 2)], z_source.at[:, 0:ROWS, :]),
        local(modx.at[pl.ds(2 * other, 2)], z_source.at[:, ROWS:EXT, :]),
    ]
    load_own = [
        local(lat.at[pl.ds(2 * zhi, 2)], rows_all.at[:, 0:ROWS, columns(tp)]),
        local(modx.at[pl.ds(2 * zhi, 2)], rows_all.at[:, ROWS:EXT, columns(tp)]),
    ]
    load_query = [
        local(wqkv.at[i], w_query.at[zhi, :, i * HD : (i + 1) * HD]) for i in range(6)
    ]
    load_cross = [
        local(wckv.at[i], w_cross.at[zhi, :, i * HD : (i + 1) * HD]) for i in range(4)
    ] + [
        local(wcq.at[i], w_cross.at[zhi, :, (4 + i) * HD : (5 + i) * HD]) for i in range(2)
    ]
    load_out = [local(wout, w_out.at[zhi])]
    load_cout = [local(wcout, w_cout.at[zhi])]
    load_table = [local(parents.at[pl.ds(zhi, 3)], table.at[pl.ds(other, 3)])]

    barrier = pltpu.get_barrier_semaphore()

    def greet(target):
        pl.semaphore_signal(barrier, inc=1, device_id=target, device_id_type=MESH)

    greet(dev(dx=1))
    greet(dev(dx=-1))
    greet(dev(dx=2))
    greet(dev(dz=4))
    greet(dev(dz=-step_z))
    greet(dev(dy=1))
    greet(dev(dy=-1))
    greet(dev(dc=1))
    greet({"grp": lax.rem(grp + 2 * zhi - 1 + 32, 32), "tp": tp})
    owner = lax.div(x, 2) == c
    own_group = lax.rem(x, 2)

    @pl.loop(0, 32)
    def _(i):
        source_c = lax.rem(i, 2)
        source_tp = (2 * source_c + lax.rem(zlo, 2)) * 2 + lax.div(zlo, 2)

        @pl.when(jnp.logical_or(i != grp, source_tp != tp))
        def _():
            greet({"grp": i, "tp": source_tp})

    to_self = (zlo == 2 * zhi + own_group).astype(jnp.int32)
    pl.semaphore_wait(barrier, 9 + owner.astype(jnp.int32) * (64 - to_self))

    def slab(group, tp_index):
        return rows_all.at[group, :, columns(tp_index)]

    for copy in load_z:
        copy.wait()
    for group in range(2):
        remote(z_source.at[group], slab(group, tp), ("z", group), dev(dz=4)).start()
    for copy in load_own:
        copy.wait()

    def spread(kind, tp_index):
        for group in range(2):
            for way in (1, -1):
                ref = slab(group, tp_index)
                remote(ref, ref, ("x", kind, group, way), dev(dx=way)).start()

    def tp_at(dx, kind):
        return lax.rem(x + dx + 4, 4) * 2 + (zhi if kind == 0 else other)

    def spread_relay(kind):
        for group, way in ((0, 1), (1, -1)):
            ref = slab(group, tp_at(-way, kind))
            arrived(ref, ("x", kind, group, way))
            remote(ref, ref, ("xr", kind, group), dev(dx=way)).start()

    def spread_end(kind):
        for group, way in ((0, -1), (1, 1)):
            arrived(slab(group, tp_at(-way, kind)), ("x", kind, group, way))
        for group in range(2):
            arrived(slab(group, tp_at(2, kind)), ("xr", kind, group))

    spread(0, tp)
    remote(
        parents.at[3 * other], table.at[3 * zhi], ("halo",),
        {"grp": lax.rem(grp + 1 - 2 * zhi + 32, 32), "tp": tp},
    ).start()

    buffers = (w_query, w_cross, w_out, w_cout)
    slice_sent = is_source * zhi + (1 - is_source) * other

    def part(which, index, quarter, core, sub=None):
        rows = WEIGHT_ROWS[which]
        start = quarter * (rows // 4) + core * (rows // 8)
        size = rows // 8
        if sub is not None:
            size = rows // 16
            start = start + sub * size
        return buffers[which].at[index, pl.ds(pl.multiple_of(start, rows // 16), size), :]

    chain_copies = {}

    def chain_prepare(which):
        for sub in range(2):
            ref = part(which, slice_sent, y, c, sub)
            chain_copies[which, sub] = remote(ref, ref, ("chain", which, sub), dev(dz=step_z))

    def chain_start(which):
        chain_prepare(which)

        @pl.when(is_source == 1)
        def _():
            for sub in range(2):
                chain_copies[which, sub].start()

    def chain_relay(which):
        for sub in range(2):
            ref = part(which, other, y, c, sub)
            arrived(ref, ("chain", which, sub))

            @pl.when(is_source == 0)
            def _():
                chain_copies[which, sub].start()

            for way in (1, -1):
                remote(ref, ref, ("y", which, sub, way), dev(dy=way)).start()

    def quarter_at(dy):
        return lax.rem(y + dy + 4, 4)

    def core_forward(which, dy):
        ref = part(which, other, quarter_at(dy), c)
        remote(ref, ref, ("core", which, dy), dev(dc=1)).start()

    def y_relay(which):
        for sub, way in ((0, 1), (1, -1)):
            ref = part(which, other, quarter_at(-way), c, sub)
            arrived(ref, ("y", which, sub, way))
            remote(ref, ref, ("yr", which, sub), dev(dy=way)).start()
        core_forward(which, 0)

    def y_end(which):
        for sub, way in ((1, 1), (0, -1)):
            arrived(part(which, other, quarter_at(-way), c, sub), ("y", which, sub, way))
            core_forward(which, -way)
        for sub in range(2):
            arrived(part(which, other, quarter_at(2), c, sub), ("yr", which, sub))
        core_forward(which, 2)
        for dy in (0, 1, -1, 2):
            arrived(part(which, other, quarter_at(dy), 1 - c), ("core", which, dy))

    for copy in load_query:
        copy.wait()
    chain_start(QUERY)

    def choose():
        for copy in load_table:
            copy.wait()
        arrived(table.at[3 * zhi], ("halo",))
        for group in range(2):
            index = grp * 4 + 2 * zhi + group
            first = pairs[2 * zhi + group, 0]
            second = pairs[2 * zhi + group, 1]
            chosen[group * 32 : group * 32 + 16, :] = jnp.where(
                first == index - 1, table[group], table[group + 1]
            )
            chosen[group * 32 + 16 : group * 32 + 32, :] = jnp.where(
                second == index + 1, table[group + 2], table[group + 1]
            )

    def fold_slice(phase, index):
        kv = jnp.dot(chosen[...], w_cross[index, :, 0:512], preferred_element_type=F32).astype(BF)
        for head in range(2):
            key = kv[:, head * HD : (head + 1) * HD]
            value = kv[:, 256 + head * HD : 256 + (head + 1) * HD]
            for n in range(4):
                cols = slice(n * 512, (n + 1) * 512)
                left = lax.dot_general(
                    key, w_cross[index, cols, 512 + head * HD : 512 + (head + 1) * HD],
                    (((1,), (1,)), ((), ())), preferred_element_type=F32,
                ) * (1.0 / math.sqrt(HD))
                right = jnp.dot(
                    value, w_cout[index, head * HD : (head + 1) * HD, cols],
                    preferred_element_type=F32,
                )
                for group in range(2):
                    there = slice(head * 32, head * 32 + 32)
                    here = slice(group * 32, group * 32 + 32)
                    fold_send[0, group, phase, there, cols] = left[here].astype(BF)
                    fold_send[1, group, phase, there, cols] = right[here].astype(BF)

    def fold_start(phase):
        index = zhi if phase == 0 else other
        base = sem_id("fold", phase, 0)
        for extra in range(1, 8):
            sem_id("fold", phase, extra)
        del base
        for group in range(2):
            for side in range(2):
                rows = pl.ds(pl.multiple_of(x * 128 + index * 64, 64), 64)
                src, dst = fold_send.at[side, group, phase], fold.at[side, rows, :]
                copy = pltpu.make_async_remote_copy(
                    src_ref=src, dst_ref=dst, send_sem=send_sem.at[sem_id("fs", phase, group, side)],
                    recv_sem=recv_sem.at[sem_id("fold", phase, 0) + x * 2 + side],
                    device_id={"grp": grp, "tp": (2 * c + group) * 2 + zhi}, device_id_type=MESH,
                )

                @pl.when(x == 2 * c + group)
                def _():
                    pltpu.make_async_copy(
                        src, dst, recv_sem.at[sem_id("fold", phase, 0) + x * 2 + side]
                    ).start()

                @pl.when(x != 2 * c + group)
                def _():
                    copy.start()

                guarded.append((x != 2 * c + group, copy))

    guarded = []

    def normalise(group):
        mod = rows_all[group, ROWS:EXT, :].astype(F32)
        shift, scale = mod[0:1], mod[1:2]

        @pl.loop(0, ROWS // 32)
        def _(i):
            rows = pl.ds(pl.multiple_of(i * 32, 32), 32)
            values = rows_all[group, rows, :].astype(F32)
            hidden[group, rows, :] = norm_rows(values, scale, shift).astype(BF)

    def attend(group):
        mod = rows_all[group, ROWS:EXT, 0:256].astype(F32)
        frame = lax.div(lax.broadcasted_iota(jnp.int32, (1, ROWS), 1), P_SIZE).astype(F32)
        keep = (frame < mod[6:7]).astype(F32)

        @pl.loop(0, 2)
        def _(s):
            for n in range(3):
                cols = slice(n * 256, (n + 1) * 256)
                qkv[:, cols] = jnp.dot(
                    hidden[group], w_query[s, :, cols], preferred_element_type=F32
                ).astype(BF)
            for head in range(2):
                cols = slice(head * HD, (head + 1) * HD)
                query = qkv[:, cols]
                key = qkv[:, 256 + head * HD : 256 + (head + 1) * HD]
                value = qkv[:, 512 + head * HD : 512 + (head + 1) * HD]
                scores = lax.dot_general(
                    query, key, (((1,), (1,)), ((), ())), preferred_element_type=F32
                ) * (1.0 / math.sqrt(HD))
                weights = jnp.exp(scores) * keep
                probs = (weights / jnp.sum(weights, axis=-1, keepdims=True)).astype(BF)
                attn[s, :, cols] = jnp.dot(probs, value, preferred_element_type=F32).astype(BF)

    def project(group):
        for n in range(4):
            cols = slice(n * 512, (n + 1) * 512)
            total = jnp.dot(attn[0], w_out[0, :, cols], preferred_element_type=F32)
            total = total + jnp.dot(attn[1], w_out[1, :, cols], preferred_element_type=F32)
            branch_send[group, :, cols] = total.astype(BF)
        src, dst = branch_send.at[group], branch_recv.at[x]
        base = sem_id("branch", 0)
        for index in range(1, 4):
            sem_id("branch", index)
        copy = pltpu.make_async_remote_copy(
            src_ref=src, dst_ref=dst, send_sem=send_sem.at[sem_id("bs", group)],
            recv_sem=recv_sem.at[base + x],
            device_id={"grp": grp, "tp": (2 * c + group) * 2 + zhi}, device_id_type=MESH,
        )

        @pl.when(x == 2 * c + group)
        def _():
            pltpu.make_async_copy(src, dst, recv_sem.at[base + x]).start()

        @pl.when(x != 2 * c + group)
        def _():
            copy.start()

        guarded.append((x != 2 * c + group, copy))

    spread_relay(0)
    chain_relay(QUERY)
    for group in range(2):
        arrived(slab(group, tp_at(0, 1)), ("z", group))
    spread(1, tp_at(0, 1))
    for copy in load_out + load_cross + load_cout:
        copy.wait()
    chain_start(OUT)
    chain_start(CROSS)
    chain_start(COUT)
    blocks[...] = (
        lax.div(lax.broadcasted_iota(jnp.int32, (512, 512), 0), 32)
        == lax.div(lax.broadcasted_iota(jnp.int32, (512, 512), 1), 32)
    ).astype(F32).astype(BF)
    choose()
    fold_slice(0, zhi)
    spread_relay(1)
    y_relay(QUERY)
    spread_end(0)
    spread_end(1)
    fold_start(0)
    normalise(0)
    chain_relay(OUT)
    normalise(1)
    y_end(QUERY)
    y_relay(OUT)
    attend(0)
    y_end(OUT)
    chain_relay(CROSS)
    project(0)
    attend(1)
    project(1)
    y_relay(CROSS)
    chain_relay(COUT)
    y_end(CROSS)
    y_relay(COUT)
    y_end(COUT)
    fold_slice(1, other)
    fold_start(1)

    def final_copy(i):
        near, far = lax.div(i, 8), lax.rem(i, 8)
        target = (2 * zhi + own_group) * 8 + near
        src = result.at[pl.ds(pl.multiple_of(near * 32, 32), 32), columns(far)]
        dst = out.at[grp]
        return target, far, src, dst, pltpu.make_async_remote_copy(
            src_ref=src, dst_ref=dst, send_sem=final_sem.at[i], recv_sem=out_sem,
            device_id={"grp": target, "tp": far}, device_id_type=MESH,
        )

    @pl.when(owner)
    def _():
        for index in range(4):
            arrived(branch_recv.at[index], ("branch", 0), index)
        mod = rows_all[own_group, ROWS:EXT, :].astype(F32)
        gate1, shift2, scale2, gate2 = mod[2:3], mod[3:4], mod[4:5], mod[5:6]

        @pl.loop(0, ROWS // 32)
        def _(i):
            rows = pl.ds(pl.multiple_of(i * 32, 32), 32)
            total = branch_recv[0, rows, :].astype(F32)
            for index in range(1, 4):
                total = total + branch_recv[index, rows, :].astype(F32)
            value = (rows_all[own_group, rows, :].astype(F32) + gate1 * total).astype(BF)
            x_one[rows, :] = value
            hidden[0, rows, :] = norm_rows(value.astype(F32), scale2, shift2).astype(BF)

        for phase in range(2):
            index = zhi if phase == 0 else other
            for source in range(4):
                rows = pl.ds(pl.multiple_of(source * 128 + index * 64, 64), 64)
                for side in range(2):
                    arrived(fold.at[side, rows, :], ("fold", phase, 0), source * 2 + side)

        @pl.loop(0, 2)
        def _(i):
            rows = pl.ds(pl.multiple_of(i * 128, 128), 128)
            scores = lax.dot_general(
                hidden[0, rows, :], fold[0], (((1,), (1,)), ((), ())), preferred_element_type=F32
            )
            weights = jnp.exp(scores).astype(BF)
            total = jnp.dot(weights, blocks[...], preferred_element_type=F32)
            probs = (weights.astype(F32) / total).astype(BF)
            for n in range(4):
                cols = slice(n * 512, (n + 1) * 512)
                branch = jnp.dot(probs, fold[1, :, cols], preferred_element_type=F32)
                result[rows, cols] = (
                    x_one[rows, cols].astype(F32) + gate2[:, cols] * branch
                ).astype(BF)

            @pl.loop(i * 32, i * 32 + 32)
            def _(j):
                target, far, src, dst, copy = final_copy(j)
                mine = jnp.logical_and(target == grp, far == tp)

                @pl.when(mine)
                def _():
                    pltpu.make_async_copy(src, dst, out_sem).start()

                @pl.when(jnp.logical_not(mine))
                def _():
                    copy.start()

    for copy in sends:
        copy.wait_send()
    for condition, copy in guarded:

        @pl.when(condition)
        def _():
            copy.wait_send()

    @pl.when(owner)
    def _():
        @pl.loop(0, 64)
        def _(j):
            target, far, src, dst, copy = final_copy(j)

            @pl.when(jnp.logical_or(target != grp, far != tp))
            def _():
                copy.wait_send()

    pltpu.make_async_remote_copy(
        src_ref=out, dst_ref=out, send_sem=send_sem.at[0], recv_sem=out_sem,
        device_id=dev(dc=1), device_id_type=MESH,
    ).wait_recv()
    assert len(names) <= 192 and locals_used[0] <= 32


def on_device(
    latents, parents, parent_pairs, timestep, valid_frames, w_mod, w_qkv, w_out, w_cq, w_ckv, w_cout
):
    groups = parent_pairs.shape[0]
    temb = embed_time(timestep)
    mod = jnp.einsum("gt,tkd->gkd", temb, w_mod, preferred_element_type=F32).astype(BF)
    valid = jnp.broadcast_to(valid_frames.astype(BF)[:, None, None], (groups, 1, 256))
    modx = jnp.concatenate([mod, valid, jnp.zeros((groups, 9, 256), BF)], axis=1)
    wqkv = w_qkv.transpose(1, 2, 0, 3).reshape(6, D, HD)
    wckv = w_ckv.transpose(1, 2, 0, 3).reshape(4, D, HD)
    wcq = w_cq.transpose(1, 0, 2)
    hbm = pl.BlockSpec(memory_space=pl.ANY)
    moved = pl.pallas_call(
        kernel,
        out_shape=jax.ShapeDtypeStruct((32, 32, 256), BF),
        in_specs=[hbm] * 8 + [pl.BlockSpec(memory_space=pltpu.SMEM)],
        out_specs=hbm,
        scratch_shapes=[
            pltpu.VMEM((2, EXT, D), BF),
            pltpu.VMEM((2, EXT, 256), BF),
            pltpu.VMEM((2, D, 768), BF),
            pltpu.VMEM((2, D, 768), BF),
            pltpu.VMEM((2, 2 * HD, D), BF),
            pltpu.VMEM((2, 2 * HD, D), BF),
            pltpu.VMEM((4, P_SIZE, D), BF),
            pltpu.VMEM((64, D), BF),
            pltpu.VMEM((2, ROWS, D), BF),
            pltpu.VMEM((ROWS, 768), BF),
            pltpu.VMEM((2, ROWS, 2 * HD), BF),
            pltpu.VMEM((2, ROWS, D), BF),
            pltpu.VMEM((4, ROWS, D), BF),
            pltpu.VMEM((2, 2, 2, 64, D), BF),
            pltpu.VMEM((2, 512, D), BF),
            pltpu.VMEM((ROWS, D), BF),
            pltpu.VMEM((ROWS, D), BF),
            pltpu.VMEM((512, 512), BF),
            pltpu.SemaphoreType.DMA((32,)),
            pltpu.SemaphoreType.DMA((192,)),
            pltpu.SemaphoreType.DMA((192,)),
            pltpu.SemaphoreType.DMA((64,)),
            pltpu.SemaphoreType.DMA,
        ],
        compiler_params=pltpu.CompilerParams(
            collective_id=0, has_side_effects=True, vmem_limit_bytes=58 << 20
        ),
        name="dit_block",
    )(
        latents.reshape(groups, ROWS, 256), modx, parents, wqkv, wckv, wcq,
        w_out.reshape(2 * HD, D), w_cout.reshape(2 * HD, D), parent_pairs,
    )
    return moved.reshape(32, 2, P_SIZE, 256)


def solution(mesh):
    in_specs = (
        P("grp", "tp"),
        P("grp", None, None),
        P("grp", None),
        P("grp"),
        P("grp"),
        P(None, None, "tp"),
        P(None, None, "tp", None),
        P("tp", None, None),
        P(None, "tp", None),
        P(None, None, "tp", None),
        P("tp", None, None),
    )
    out_specs = P(None, "grp", None, "tp")
    return jax.shard_map(
        on_device, mesh=mesh, in_specs=in_specs, out_specs=out_specs, check_vma=False
    )
```

```python
import math

import jax
import jax.numpy as jnp
from jax import lax
from jax.experimental import pallas as pl
from jax.experimental.pallas import tpu as pltpu
from jax.sharding import PartitionSpec as P

D = 2048
HD = 128
TEMB = 256
F = 16
P_SIZE = 16
ROWS = F * P_SIZE
EXT = ROWS + 16
MESH = pl.DeviceIdType.MESH
BF = jnp.bfloat16
F32 = jnp.float32
KEYS, VALUES, CROSS, OUT, COUT = range(5)
WEIGHT_ROWS = (D, D, D, 2 * HD, 2 * HD)


def embed_time(stamp):
    half = TEMB // 2
    freq = jnp.exp(-math.log(10000.0) * jnp.arange(half, dtype=jnp.float32) / half)
    angle = stamp.astype(jnp.float32)[..., None] * freq
    return jax.nn.silu(jnp.concatenate([jnp.cos(angle), jnp.sin(angle)], axis=-1)).astype(BF)


def norm_rows(values, scale, shift):
    centre = values - jnp.mean(values, axis=-1, keepdims=True)
    spread = jnp.mean(centre * centre, axis=-1, keepdims=True)
    return centre * lax.rsqrt(spread + 1e-06) * (1.0 + scale) + shift


def kernel(
    lat, modx, parents, wqkv, wckv, wcq, wout, wcout, pairs, out,
    rows_all, z_source, w_query, w_cross, w_out, w_cout, w_kv, table, chosen, kv_own, kv_other, hidden, qkv, attn,
    branch_send, branch_recv, fold_send, fold, x_one, result, blocks,
    local_sem, send_sem, recv_sem, final_sem, out_sem,
):
    grp, tp = lax.axis_index("grp"), lax.axis_index("tp")
    c, y, zlo = lax.rem(grp, 2), lax.rem(lax.div(grp, 2), 4), lax.div(grp, 8)
    x, zhi = lax.div(tp, 2), lax.rem(tp, 2)
    z = zhi * 4 + zlo
    other = 1 - zhi
    step_z = 1 - 2 * c
    place = c * 3 + step_z * zlo
    is_source = lax.div(place, 3)

    def group_at(half, index):
        return (1 - half) * 3 * index + half * (1 + index)

    def dev(dx=0, dy=0, dz=0, dc=0):
        xx, yy = lax.rem(x + dx + 4, 4), lax.rem(y + dy + 4, 4)
        zz, cc = lax.rem(z + dz + 8, 8), lax.rem(c + dc, 2)
        return {
            "grp": (lax.rem(zz, 4) * 4 + yy) * 2 + cc,
            "tp": xx * 2 + lax.div(zz, 4),
        }

    names = {}

    def sem_id(*name):
        return names.setdefault(name, len(names))

    sends = []

    def remote(src, dst, name, target, extra=0, note=True):
        copy = pltpu.make_async_remote_copy(
            src_ref=src, dst_ref=dst, send_sem=send_sem.at[sem_id(*name)],
            recv_sem=recv_sem.at[sem_id(*name) + extra], device_id=target, device_id_type=MESH,
        )
        if note:
            sends.append(copy)
        return copy

    def arrived(region, name, extra=0):
        pltpu.make_async_remote_copy(
            src_ref=region, dst_ref=region, send_sem=send_sem.at[0],
            recv_sem=recv_sem.at[sem_id(*name) + extra], device_id=dev(dc=1), device_id_type=MESH,
        ).wait_recv()

    locals_used = [0]

    def local(src, dst):
        copy = pltpu.make_async_copy(src, dst, local_sem.at[locals_used[0]])
        locals_used[0] += 1
        copy.start()
        return copy

    def columns(index):
        return pl.ds(pl.multiple_of(index * 256, 256), 256)

    load_z, load_own = [], []
    for group in range(2):
        there, here = group_at(other, group), group_at(zhi, group)
        load_z.append(local(lat.at[there], z_source.at[group, 0:ROWS, :]))
        load_z.append(local(modx.at[there], z_source.at[group, ROWS:EXT, :]))
        load_own.append(local(lat.at[here], rows_all.at[group, 0:ROWS, columns(tp)]))
        load_own.append(local(modx.at[here], rows_all.at[group, ROWS:EXT, columns(tp)]))
    load_query = [
        local(wqkv.at[i], w_query.at[zhi, :, i * HD : (i + 1) * HD]) for i in range(6)
    ]
    load_cross = [
        local(wcq.at[i], w_cross.at[zhi, :, i * HD : (i + 1) * HD]) for i in range(2)
    ]
    load_cout = [local(wcout, w_cout.at[zhi])]
    load_out = [local(wout, w_out.at[zhi])]
    load_kv = [local(wckv.at[i], w_kv.at[:, i * HD : (i + 1) * HD]) for i in range(4)]
    load_table = [local(parents, table.at[1:5])]

    barrier = pltpu.get_barrier_semaphore()

    def grp_at(step):
        return {"grp": lax.rem(grp + step + 32, 32), "tp": tp}

    def greet(target):
        pl.semaphore_signal(barrier, inc=1, device_id=target, device_id_type=MESH)

    greet(dev(dx=1))
    greet(dev(dx=-1))
    greet(dev(dx=2))
    greet(dev(dz=4))
    greet(dev(dz=-step_z))
    greet(dev(dy=1))
    greet(dev(dy=-1))
    greet(dev(dy=2))
    greet(dev(dc=1))
    greet(grp_at(1))
    greet(grp_at(-1))
    owner = lax.div(x, 2) == c
    own_group = lax.rem(x, 2)

    @pl.loop(0, 32)
    def _(i):
        source_c = lax.rem(i, 2)
        source_tp = (2 * source_c + lax.div(zlo, 2)) * 2 + lax.rem(zlo + lax.div(zlo, 2), 2)

        @pl.when(jnp.logical_or(i != grp, source_tp != tp))
        def _():
            greet({"grp": i, "tp": source_tp})

    to_self = (zlo == group_at(zhi, own_group)).astype(jnp.int32)
    pl.semaphore_wait(barrier, 11 + owner.astype(jnp.int32) * (64 - to_self))

    def slab(group, tp_index):
        return rows_all.at[group, :, columns(tp_index)]

    def spread(kind, tp_index):
        for group in range(2):
            for way in (1, -1):
                ref = slab(group, tp_index)
                remote(ref, ref, ("x", kind, group, way), dev(dx=way)).start()

    def tp_at(dx, kind):
        return lax.rem(x + dx + 4, 4) * 2 + (zhi if kind == 0 else other)

    def spread_relay(kind):
        for group, way in ((0, 1), (1, -1)):
            ref = slab(group, tp_at(-way, kind))
            arrived(ref, ("x", kind, group, way))
            remote(ref, ref, ("xr", kind, group), dev(dx=way)).start()

    def spread_end(kind):
        for group, way in ((0, -1), (1, 1)):
            arrived(slab(group, tp_at(-way, kind)), ("x", kind, group, way))
        for group in range(2):
            arrived(slab(group, tp_at(2, kind)), ("xr", kind, group))

    buffers = (w_query, w_query, w_cross, w_out, w_cout)
    widths = (slice(0, 512), slice(512, 768), slice(0, 256), slice(0, D), slice(0, D))
    slice_sent = is_source * zhi + (1 - is_source) * other

    def part(which, index, quarter, core, sub=None):
        rows = WEIGHT_ROWS[which]
        size = rows // 8
        start = quarter * (rows // 4) + core * size
        if sub is not None:
            size = size // 2
            start = start + sub * size
        there = pl.ds(pl.multiple_of(start, rows // 16), size)
        return buffers[which].at[index, there, widths[which]]

    chain_copies = {}

    def chain_prepare(which):
        for sub in range(2):
            ref = part(which, slice_sent, y, c, sub)
            chain_copies[which, sub] = remote(ref, ref, ("chain", which, sub), dev(dz=step_z))

    def chain_start(which):
        chain_prepare(which)

        @pl.when(is_source == 1)
        def _():
            for sub in range(2):
                chain_copies[which, sub].start()

    def chain_relay(which):
        for sub in range(2):
            ref = part(which, other, y, c, sub)
            arrived(ref, ("chain", which, sub))

            @pl.when(is_source == 0)
            def _():
                chain_copies[which, sub].start()

            for way in (1, -1, 2):
                remote(ref, ref, ("y", which, sub, way), dev(dy=way)).start()

    def quarter_at(dy):
        return lax.rem(y + dy + 4, 4)

    def core_forward(which, dy):
        ref = part(which, other, quarter_at(dy), c)
        remote(ref, ref, ("core", which, dy), dev(dc=1)).start()

    def y_middle(which):
        core_forward(which, 0)
        for way in (1, -1, 2):
            for sub in range(2):
                arrived(part(which, other, quarter_at(-way), c, sub), ("y", which, sub, way))
            core_forward(which, -way)

    def y_end(which):
        for dy in (0, 1, -1, -2):
            arrived(part(which, other, quarter_at(dy), 1 - c), ("core", which, dy))

    def choose():
        for copy in load_table:
            copy.wait()
        arrived(table.at[0], ("halo", 1))
        arrived(table.at[5], ("halo", -1))
        for place_at in range(4):
            group = group_at(zhi if place_at < 2 else other, place_at % 2)
            index = grp * 4 + group
            rows = place_at * 32
            chosen[rows : rows + 16, :] = jnp.where(
                pairs[group, 0] == index - 1, table[group], table[group + 1]
            )
            chosen[rows + 16 : rows + 32, :] = jnp.where(
                pairs[group, 1] == index + 1, table[group + 2], table[group + 1]
            )
        for copy in load_kv:
            copy.wait()
        kv_own[...] = jnp.dot(chosen[...], w_kv[...], preferred_element_type=F32).astype(BF)
        remote(kv_own.at[64:128], kv_other, ("kv",), dev(dz=4)).start()

    def fold_slice(phase, index):
        if phase == 0:
            kv = kv_own[0:64, :]
        else:
            arrived(kv_other, ("kv",))
            kv = kv_other[...]
        for head in range(2):
            key = kv[:, head * HD : (head + 1) * HD]
            value = kv[:, 256 + head * HD : 256 + (head + 1) * HD]
            for n in range(4):
                cols = slice(n * 512, (n + 1) * 512)
                left = lax.dot_general(
                    key, w_cross[index, cols, head * HD : (head + 1) * HD],
                    (((1,), (1,)), ((), ())), preferred_element_type=F32,
                ) * (1.0 / math.sqrt(HD))
                right = jnp.dot(
                    value, w_cout[index, head * HD : (head + 1) * HD, cols],
                    preferred_element_type=F32,
                )
                for group in range(2):
                    there = slice(head * 32, head * 32 + 32)
                    here = slice(group * 32, group * 32 + 32)
                    fold_send[0, group, phase, there, cols] = left[here].astype(BF)
                    fold_send[1, group, phase, there, cols] = right[here].astype(BF)

    def fold_start(phase):
        index = zhi if phase == 0 else other
        for extra in range(8):
            sem_id("fold", phase, extra)
        for group in range(2):
            for side in range(2):
                rows = pl.ds(pl.multiple_of(x * 128 + index * 64, 64), 64)
                src, dst = fold_send.at[side, group, phase], fold.at[side, rows, :]
                copy = pltpu.make_async_remote_copy(
                    src_ref=src, dst_ref=dst, send_sem=send_sem.at[sem_id("fs", phase, group, side)],
                    recv_sem=recv_sem.at[sem_id("fold", phase, 0) + x * 2 + side],
                    device_id={"grp": grp, "tp": (2 * c + group) * 2 + zhi}, device_id_type=MESH,
                )

                @pl.when(x == 2 * c + group)
                def _():
                    pltpu.make_async_copy(
                        src, dst, recv_sem.at[sem_id("fold", phase, 0) + x * 2 + side]
                    ).start()

                @pl.when(x != 2 * c + group)
                def _():
                    copy.start()

                guarded.append((x != 2 * c + group, copy))

    guarded = []

    def normalise(group):
        mod = rows_all[group, ROWS:EXT, :].astype(F32)
        shift, scale = mod[0:1], mod[1:2]

        @pl.loop(0, ROWS // 32)
        def _(i):
            rows = pl.ds(pl.multiple_of(i * 32, 32), 32)
            values = rows_all[group, rows, :].astype(F32)
            hidden[group, rows, :] = norm_rows(values, scale, shift).astype(BF)

    def attend(group, s):
        mod = rows_all[group, ROWS:EXT, 0:256].astype(F32)
        frame = lax.div(lax.broadcasted_iota(jnp.int32, (1, ROWS), 1), P_SIZE).astype(F32)
        keep = (frame < mod[6:7]).astype(F32)

        for n in range(3):
            cols = slice(n * 256, (n + 1) * 256)
            qkv[:, cols] = jnp.dot(
                hidden[group], w_query[s, :, cols], preferred_element_type=F32
            ).astype(BF)
        for head in range(2):
            cols = slice(head * HD, (head + 1) * HD)
            query = qkv[:, cols]
            key = qkv[:, 256 + head * HD : 256 + (head + 1) * HD]
            value = qkv[:, 512 + head * HD : 512 + (head + 1) * HD]
            scores = lax.dot_general(
                query, key, (((1,), (1,)), ((), ())), preferred_element_type=F32
            ) * (1.0 / math.sqrt(HD))
            weights = jnp.exp(scores) * keep
            probs = (weights / jnp.sum(weights, axis=-1, keepdims=True)).astype(BF)
            attn[group, s, :, cols] = jnp.dot(probs, value, preferred_element_type=F32).astype(BF)

    def project(group):
        for n in range(4):
            cols = slice(n * 512, (n + 1) * 512)
            total = jnp.dot(attn[group, 0], w_out[0, :, cols], preferred_element_type=F32)
            total = total + jnp.dot(attn[group, 1], w_out[1, :, cols], preferred_element_type=F32)
            branch_send[group, :, cols] = total.astype(BF)
    def branch_copy(group, half):
        rows = pl.ds(half * 128, 128)
        src, dst = branch_send.at[group, rows, :], branch_recv.at[x, rows, :]
        for index in range(4):
            sem_id("branch", half, index)
        slot = sem_id("branch", half, 0) + x
        return src, dst, slot, pltpu.make_async_remote_copy(
            src_ref=src, dst_ref=dst, send_sem=send_sem.at[sem_id("bs", group, half)],
            recv_sem=recv_sem.at[slot],
            device_id={"grp": grp, "tp": (2 * c + group) * 2 + zhi}, device_id_type=MESH,
        )

    def branch_start(group, half):
        src, dst, slot, copy = branch_copy(group, half)

        @pl.when(x == 2 * c + group)
        def _():
            pltpu.make_async_copy(src, dst, recv_sem.at[slot]).start()

        @pl.when(x != 2 * c + group)
        def _():
            copy.start()

    def branch_sent(group, half):
        copy = branch_copy(group, half)[3]

        @pl.when(x != 2 * c + group)
        def _():
            copy.wait_send()

    def ready(copies):
        for copy in copies:
            copy.wait()

    ready(load_z)
    for group in range(2):
        remote(z_source.at[group], slab(group, tp), ("z", group), dev(dz=4)).start()
    ready(load_own)
    spread(0, tp)
    remote(parents.at[3], table.at[0], ("halo", 1), grp_at(1)).start()
    remote(parents.at[0], table.at[5], ("halo", -1), grp_at(-1)).start()
    ready(load_cross)
    chain_start(CROSS)
    ready(load_cout)
    chain_start(COUT)
    ready(load_query)
    chain_start(KEYS)
    ready(load_out)
    chain_start(VALUES)
    chain_start(OUT)
    choose()
    spread_relay(0)
    chain_relay(CROSS)
    chain_relay(COUT)
    chain_relay(KEYS)
    fold_slice(0, zhi)
    fold_start(0)
    for group in range(2):
        arrived(slab(group, tp_at(0, 1)), ("z", group))
    spread(1, tp_at(0, 1))
    chain_relay(VALUES)
    chain_relay(OUT)
    y_middle(CROSS)
    y_middle(COUT)
    spread_relay(1)
    y_middle(KEYS)
    y_end(CROSS)
    y_end(COUT)
    fold_slice(1, other)
    fold_start(1)
    spread_end(0)
    spread_end(1)
    normalise(0)
    y_middle(VALUES)
    normalise(1)
    attend(0, zhi)
    y_middle(OUT)
    attend(1, zhi)
    y_end(KEYS)
    y_end(VALUES)
    attend(0, other)
    y_end(OUT)
    project(0)
    branch_start(0, 0)
    attend(1, other)
    project(1)
    branch_start(1, 0)
    branch_sent(0, 0)
    branch_start(0, 1)
    branch_sent(1, 0)
    branch_start(1, 1)
    blocks[...] = (
        lax.div(lax.broadcasted_iota(jnp.int32, (512, 512), 0), 32)
        == lax.div(lax.broadcasted_iota(jnp.int32, (512, 512), 1), 32)
    ).astype(F32).astype(BF)

    def final_copy(i):
        near, far = lax.div(i, 8), lax.rem(i, 8)
        target = group_at(zhi, own_group) * 8 + near
        src = result.at[pl.ds(pl.multiple_of(near * 32, 32), 32), columns(far)]
        dst = out.at[grp]
        return target, far, src, dst, pltpu.make_async_remote_copy(
            src_ref=src, dst_ref=dst, send_sem=final_sem.at[i], recv_sem=out_sem,
            device_id={"grp": target, "tp": far}, device_id_type=MESH,
        )

    @pl.when(owner)
    def _():
        mod = rows_all[own_group, ROWS:EXT, :].astype(F32)
        gate1, shift2, scale2, gate2 = mod[2:3], mod[3:4], mod[4:5], mod[5:6]
        for half in range(2):
            for index in range(4):
                arrived(
                    branch_recv.at[index, pl.ds(half * 128, 128), :], ("branch", half, 0), index
                )

            @pl.loop(0, 4)
            def _(i):
                rows = pl.ds(pl.multiple_of(half * 128 + i * 32, 32), 32)
                total = branch_recv[0, rows, :].astype(F32)
                for index in range(1, 4):
                    total = total + branch_recv[index, rows, :].astype(F32)
                value = (rows_all[own_group, rows, :].astype(F32) + gate1 * total).astype(BF)
                x_one[rows, :] = value
                hidden[0, rows, :] = norm_rows(value.astype(F32), scale2, shift2).astype(BF)

            for phase in range(2 if half == 0 else 0):
                index = zhi if phase == 0 else other
                for source in range(4):
                    rows = pl.ds(pl.multiple_of(source * 128 + index * 64, 64), 64)
                    for side in range(2):
                        arrived(fold.at[side, rows, :], ("fold", phase, 0), source * 2 + side)

            rows = pl.ds(half * 128, 128)
            scores = lax.dot_general(
                hidden[0, rows, :], fold[0], (((1,), (1,)), ((), ())), preferred_element_type=F32
            )
            weights = jnp.exp(scores).astype(BF)
            total = jnp.dot(weights, blocks[...], preferred_element_type=F32)
            probs = (weights.astype(F32) / total).astype(BF)
            for n in range(4):
                cols = slice(n * 512, (n + 1) * 512)
                branch = jnp.dot(probs, fold[1, :, cols], preferred_element_type=F32)
                result[rows, cols] = (
                    x_one[rows, cols].astype(F32) + gate2[:, cols] * branch
                ).astype(BF)

            @pl.loop(half * 32, half * 32 + 32)
            def _(j):
                target, far, src, dst, copy = final_copy(j)
                mine = jnp.logical_and(target == grp, far == tp)

                @pl.when(mine)
                def _():
                    pltpu.make_async_copy(src, dst, out_sem).start()

                @pl.when(jnp.logical_not(mine))
                def _():
                    copy.start()

    for copy in sends:
        copy.wait_send()
    for condition, copy in guarded:

        @pl.when(condition)
        def _():
            copy.wait_send()

    branch_sent(0, 1)
    branch_sent(1, 1)

    @pl.when(owner)
    def _():
        @pl.loop(0, 64)
        def _(j):
            target, far, src, dst, copy = final_copy(j)

            @pl.when(jnp.logical_or(target != grp, far != tp))
            def _():
                copy.wait_send()

    pltpu.make_async_remote_copy(
        src_ref=out, dst_ref=out, send_sem=send_sem.at[0], recv_sem=out_sem,
        device_id=dev(dc=1), device_id_type=MESH,
    ).wait_recv()
    assert len(names) <= 192 and locals_used[0] <= 32


def on_device(
    latents, parents, parent_pairs, timestep, valid_frames, w_mod, w_qkv, w_out, w_cq, w_ckv, w_cout
):
    groups = parent_pairs.shape[0]
    temb = embed_time(timestep)
    mod = jnp.einsum("gt,tkd->gkd", temb, w_mod, preferred_element_type=F32).astype(BF)
    valid = jnp.broadcast_to(valid_frames.astype(BF)[:, None, None], (groups, 1, 256))
    modx = jnp.concatenate([mod, valid, jnp.zeros((groups, 9, 256), BF)], axis=1)
    wqkv = w_qkv.transpose(1, 2, 0, 3).reshape(6, D, HD)
    wckv = w_ckv.transpose(1, 2, 0, 3).reshape(4, D, HD)
    wcq = w_cq.transpose(1, 0, 2)
    hbm = pl.BlockSpec(memory_space=pl.ANY)
    moved = pl.pallas_call(
        kernel,
        out_shape=jax.ShapeDtypeStruct((32, 32, 256), BF),
        in_specs=[hbm] * 8 + [pl.BlockSpec(memory_space=pltpu.SMEM)],
        out_specs=hbm,
        scratch_shapes=[
            pltpu.VMEM((2, EXT, D), BF),
            pltpu.VMEM((2, EXT, 256), BF),
            pltpu.VMEM((2, D, 768), BF),
            pltpu.VMEM((2, D, 256), BF),
            pltpu.VMEM((2, 2 * HD, D), BF),
            pltpu.VMEM((2, 2 * HD, D), BF),
            pltpu.VMEM((D, 512), BF),
            pltpu.VMEM((6, P_SIZE, D), BF),
            pltpu.VMEM((128, D), BF),
            pltpu.VMEM((128, 512), BF),
            pltpu.VMEM((64, 512), BF),
            pltpu.VMEM((2, ROWS, D), BF),
            pltpu.VMEM((ROWS, 768), BF),
            pltpu.VMEM((2, 2, ROWS, 2 * HD), BF),
            pltpu.VMEM((2, ROWS, D), BF),
            pltpu.VMEM((4, ROWS, D), BF),
            pltpu.VMEM((2, 2, 2, 64, D), BF),
            pltpu.VMEM((2, 512, D), BF),
            pltpu.VMEM((ROWS, D), BF),
            pltpu.VMEM((ROWS, D), BF),
            pltpu.VMEM((512, 512), BF),
            pltpu.SemaphoreType.DMA((32,)),
            pltpu.SemaphoreType.DMA((192,)),
            pltpu.SemaphoreType.DMA((192,)),
            pltpu.SemaphoreType.DMA((64,)),
            pltpu.SemaphoreType.DMA,
        ],
        compiler_params=pltpu.CompilerParams(
            collective_id=0, has_side_effects=True, vmem_limit_bytes=58 << 20
        ),
        name="dit_block",
    )(
        latents.reshape(groups, ROWS, 256), modx, parents, wqkv, wckv, wcq,
        w_out.reshape(2 * HD, D), w_cout.reshape(2 * HD, D), parent_pairs,
    )
    return moved.reshape(32, 2, P_SIZE, 256)


def solution(mesh):
    in_specs = (
        P("grp", "tp"),
        P("grp", None, None),
        P("grp", None),
        P("grp"),
        P("grp"),
        P(None, None, "tp"),
        P(None, None, "tp", None),
        P("tp", None, None),
        P(None, "tp", None),
        P(None, None, "tp", None),
        P("tp", None, None),
    )
    out_specs = P(None, "grp", None, "tp")
    return jax.shard_map(
        on_device, mesh=mesh, in_specs=in_specs, out_specs=out_specs, check_vma=False
    )
```

```python
import math

import jax
import jax.numpy as jnp
from jax import lax
from jax.experimental import pallas as pl
from jax.experimental.pallas import tpu as pltpu
from jax.sharding import PartitionSpec as P

D = 2048
HD = 128
TEMB = 256
F = 16
P_SIZE = 16
ROWS = F * P_SIZE
EXT = ROWS + 16
MESH = pl.DeviceIdType.MESH
BF = jnp.bfloat16
F32 = jnp.float32
KEYS, VALUES, CROSS, OUT, COUT = range(5)
WEIGHT_ROWS = (D, D, D, 2 * HD, 2 * HD)


def embed_time(stamp):
    half = TEMB // 2
    freq = jnp.exp(-math.log(10000.0) * jnp.arange(half, dtype=jnp.float32) / half)
    angle = stamp.astype(jnp.float32)[..., None] * freq
    return jax.nn.silu(jnp.concatenate([jnp.cos(angle), jnp.sin(angle)], axis=-1)).astype(BF)


def norm_rows(values, scale, shift):
    centre = values - jnp.mean(values, axis=-1, keepdims=True)
    spread = jnp.mean(centre * centre, axis=-1, keepdims=True)
    return centre * lax.rsqrt(spread + 1e-06) * (1.0 + scale) + shift


def kernel(
    lat, modx, parents, wqkv, wckv, wcq, wout, wcout, pairs, out,
    rows_all, z_source, w_query, w_cross, w_out, w_cout, w_kv, table, chosen, kv_own, kv_other, hidden, qkv, attn,
    branch_send, branch_recv, fold_send, fold, x_one, result, blocks,
    local_sem, send_sem, recv_sem, final_sem, out_sem,
):
    grp, tp = lax.axis_index("grp"), lax.axis_index("tp")
    c, y, zlo = lax.rem(grp, 2), lax.rem(lax.div(grp, 2), 4), lax.div(grp, 8)
    x, zhi = lax.div(tp, 2), lax.rem(tp, 2)
    z = zhi * 4 + zlo
    other = 1 - zhi
    step_z = 1 - 2 * c
    place = c * 3 + step_z * zlo
    is_source = lax.div(place, 3)

    def group_at(half, index):
        return (1 - half) * 3 * index + half * (1 + index)

    def dev(dx=0, dy=0, dz=0, dc=0):
        xx, yy = lax.rem(x + dx + 4, 4), lax.rem(y + dy + 4, 4)
        zz, cc = lax.rem(z + dz + 8, 8), lax.rem(c + dc, 2)
        return {
            "grp": (lax.rem(zz, 4) * 4 + yy) * 2 + cc,
            "tp": xx * 2 + lax.div(zz, 4),
        }

    names = {}

    def sem_id(*name):
        return names.setdefault(name, len(names))

    sends = []

    def remote(src, dst, name, target, extra=0, note=True):
        copy = pltpu.make_async_remote_copy(
            src_ref=src, dst_ref=dst, send_sem=send_sem.at[sem_id(*name)],
            recv_sem=recv_sem.at[sem_id(*name) + extra], device_id=target, device_id_type=MESH,
        )
        if note:
            sends.append(copy)
        return copy

    def arrived(region, name, extra=0):
        pltpu.make_async_remote_copy(
            src_ref=region, dst_ref=region, send_sem=send_sem.at[0],
            recv_sem=recv_sem.at[sem_id(*name) + extra], device_id=dev(dc=1), device_id_type=MESH,
        ).wait_recv()

    locals_used = [0]

    def local(src, dst):
        copy = pltpu.make_async_copy(src, dst, local_sem.at[locals_used[0]])
        locals_used[0] += 1
        copy.start()
        return copy

    def columns(index):
        return pl.ds(pl.multiple_of(index * 256, 256), 256)

    load_z, load_own = [], []
    for group in range(2):
        there, here = group_at(other, group), group_at(zhi, group)
        load_z.append(local(lat.at[there], z_source.at[group, 0:ROWS, :]))
        load_z.append(local(modx.at[there], z_source.at[group, ROWS:EXT, :]))
        load_own.append(local(lat.at[here], rows_all.at[group, 0:ROWS, columns(tp)]))
        load_own.append(local(modx.at[here], rows_all.at[group, ROWS:EXT, columns(tp)]))
    load_query = [
        local(wqkv.at[i], w_query.at[zhi, :, i * HD : (i + 1) * HD]) for i in range(6)
    ]
    load_cross = [
        local(wcq.at[i], w_cross.at[zhi, :, i * HD : (i + 1) * HD]) for i in range(2)
    ]
    load_cout = [local(wcout, w_cout.at[zhi])]
    load_out = [local(wout, w_out.at[zhi])]
    load_kv = [local(wckv.at[i], w_kv.at[:, i * HD : (i + 1) * HD]) for i in range(4)]
    load_table = [local(parents, table.at[1:5])]

    barrier = pltpu.get_barrier_semaphore()

    def grp_at(step):
        return {"grp": lax.rem(grp + step + 32, 32), "tp": tp}

    def greet(target):
        pl.semaphore_signal(barrier, inc=1, device_id=target, device_id_type=MESH)

    greet(dev(dx=1))
    greet(dev(dx=-1))
    greet(dev(dx=2))
    greet(dev(dz=4))
    greet(dev(dz=-step_z))
    greet(dev(dy=1))
    greet(dev(dy=-1))
    greet(dev(dy=2))
    greet(dev(dc=1))
    greet(grp_at(1))
    greet(grp_at(-1))
    owner = lax.div(x, 2) == c
    own_group = lax.rem(x, 2)

    @pl.loop(0, 32)
    def _(i):
        source_c = lax.rem(i, 2)
        source_tp = (2 * source_c + lax.div(zlo, 2)) * 2 + lax.rem(zlo + lax.div(zlo, 2), 2)

        @pl.when(jnp.logical_or(i != grp, source_tp != tp))
        def _():
            greet({"grp": i, "tp": source_tp})

    to_self = (zlo == group_at(zhi, own_group)).astype(jnp.int32)
    pl.semaphore_wait(barrier, 11 + owner.astype(jnp.int32) * (64 - to_self))

    def slab(group, tp_index):
        return rows_all.at[group, :, columns(tp_index)]

    def spread(kind, tp_index):
        for group in range(2):
            for way in (1, -1):
                ref = slab(group, tp_index)
                remote(ref, ref, ("x", kind, group, way), dev(dx=way)).start()

    def tp_at(dx, kind):
        return lax.rem(x + dx + 4, 4) * 2 + (zhi if kind == 0 else other)

    def spread_relay(kind):
        for group, way in ((0, 1), (1, -1)):
            ref = slab(group, tp_at(-way, kind))
            arrived(ref, ("x", kind, group, way))
            remote(ref, ref, ("xr", kind, group), dev(dx=way)).start()

    def spread_end(kind):
        for group, way in ((0, -1), (1, 1)):
            arrived(slab(group, tp_at(-way, kind)), ("x", kind, group, way))
        for group in range(2):
            arrived(slab(group, tp_at(2, kind)), ("xr", kind, group))

    buffers = (w_query, w_query, w_cross, w_out, w_cout)
    widths = (slice(0, 512), slice(512, 768), slice(0, 256), slice(0, D), slice(0, D))
    slice_sent = is_source * zhi + (1 - is_source) * other

    def part(which, index, quarter, core, sub=None):
        rows = WEIGHT_ROWS[which]
        size = rows // 8
        start = quarter * (rows // 4) + core * size
        if sub is not None:
            size = size // 2
            start = start + sub * size
        there = pl.ds(pl.multiple_of(start, rows // 16), size)
        return buffers[which].at[index, there, widths[which]]

    chain_copies = {}

    def chain_prepare(which):
        for sub in range(2):
            ref = part(which, slice_sent, y, c, sub)
            chain_copies[which, sub] = remote(ref, ref, ("chain", which, sub), dev(dz=step_z))

    def chain_start(which):
        chain_prepare(which)

        @pl.when(is_source == 1)
        def _():
            for sub in range(2):
                chain_copies[which, sub].start()

    def chain_relay(which):
        for sub in range(2):
            ref = part(which, other, y, c, sub)
            arrived(ref, ("chain", which, sub))

            @pl.when(is_source == 0)
            def _():
                chain_copies[which, sub].start()

            for way in (1, -1, 2):
                remote(ref, ref, ("y", which, sub, way), dev(dy=way)).start()

    def quarter_at(dy):
        return lax.rem(y + dy + 4, 4)

    def core_forward(which, dy):
        ref = part(which, other, quarter_at(dy), c)
        remote(ref, ref, ("core", which, dy), dev(dc=1)).start()

    def y_middle(which):
        core_forward(which, 0)
        for way in (1, -1, 2):
            for sub in range(2):
                arrived(part(which, other, quarter_at(-way), c, sub), ("y", which, sub, way))
            core_forward(which, -way)

    def y_end(which):
        for dy in (0, 1, -1, -2):
            arrived(part(which, other, quarter_at(dy), 1 - c), ("core", which, dy))

    def choose():
        for copy in load_table:
            copy.wait()
        arrived(table.at[0], ("halo", 1))
        arrived(table.at[5], ("halo", -1))
        for place_at in range(4):
            group = group_at(zhi if place_at < 2 else other, place_at % 2)
            index = grp * 4 + group
            rows = place_at * 32
            chosen[rows : rows + 16, :] = jnp.where(
                pairs[group, 0] == index - 1, table[group], table[group + 1]
            )
            chosen[rows + 16 : rows + 32, :] = jnp.where(
                pairs[group, 1] == index + 1, table[group + 2], table[group + 1]
            )
        for copy in load_kv:
            copy.wait()
        kv_own[...] = jnp.dot(chosen[...], w_kv[...], preferred_element_type=F32).astype(BF)
        remote(kv_own.at[64:128], kv_other, ("kv",), dev(dz=4)).start()

    def fold_slice(phase, index):
        if phase == 0:
            kv = kv_own[0:64, :]
        else:
            arrived(kv_other, ("kv",))
            kv = kv_other[...]
        for head in range(2):
            key = kv[:, head * HD : (head + 1) * HD]
            value = kv[:, 256 + head * HD : 256 + (head + 1) * HD]
            for n in range(4):
                cols = slice(n * 512, (n + 1) * 512)
                left = lax.dot_general(
                    key, w_cross[index, cols, head * HD : (head + 1) * HD],
                    (((1,), (1,)), ((), ())), preferred_element_type=F32,
                ) * (1.0 / math.sqrt(HD))
                right = jnp.dot(
                    value, w_cout[index, head * HD : (head + 1) * HD, cols],
                    preferred_element_type=F32,
                )
                for group in range(2):
                    there = slice(head * 32, head * 32 + 32)
                    here = slice(group * 32, group * 32 + 32)
                    fold_send[0, group, phase, there, cols] = left[here].astype(BF)
                    fold_send[1, group, phase, there, cols] = right[here].astype(BF)

    def fold_start(phase):
        index = zhi if phase == 0 else other
        for extra in range(8):
            sem_id("fold", phase, extra)
        for group in range(2):
            for side in range(2):
                rows = pl.ds(pl.multiple_of(x * 128 + index * 64, 64), 64)
                src, dst = fold_send.at[side, group, phase], fold.at[side, rows, :]
                copy = pltpu.make_async_remote_copy(
                    src_ref=src, dst_ref=dst, send_sem=send_sem.at[sem_id("fs", phase, group, side)],
                    recv_sem=recv_sem.at[sem_id("fold", phase, 0) + x * 2 + side],
                    device_id={"grp": grp, "tp": (2 * c + group) * 2 + zhi}, device_id_type=MESH,
                )

                @pl.when(x == 2 * c + group)
                def _():
                    pltpu.make_async_copy(
                        src, dst, recv_sem.at[sem_id("fold", phase, 0) + x * 2 + side]
                    ).start()

                @pl.when(x != 2 * c + group)
                def _():
                    copy.start()

                guarded.append((x != 2 * c + group, copy))

    guarded = []

    def normalise(group):
        mod = rows_all[group, ROWS:EXT, :].astype(F32)
        shift, scale = mod[0:1], mod[1:2]

        @pl.loop(0, ROWS // 32)
        def _(i):
            rows = pl.ds(pl.multiple_of(i * 32, 32), 32)
            values = rows_all[group, rows, :].astype(F32)
            hidden[group, rows, :] = norm_rows(values, scale, shift).astype(BF)

    def attend(group, s):
        mod = rows_all[group, ROWS:EXT, 0:256].astype(F32)
        frame = lax.div(lax.broadcasted_iota(jnp.int32, (1, ROWS), 1), P_SIZE).astype(F32)
        keep = (frame < mod[6:7]).astype(F32)

        for n in range(3):
            cols = slice(n * 256, (n + 1) * 256)
            qkv[:, cols] = jnp.dot(
                hidden[group], w_query[s, :, cols], preferred_element_type=F32
            ).astype(BF)
        for head in range(2):
            cols = slice(head * HD, (head + 1) * HD)
            query = qkv[:, cols]
            key = qkv[:, 256 + head * HD : 256 + (head + 1) * HD]
            value = qkv[:, 512 + head * HD : 512 + (head + 1) * HD]
            scores = lax.dot_general(
                query, key, (((1,), (1,)), ((), ())), preferred_element_type=F32
            ) * (1.0 / math.sqrt(HD))
            weights = jnp.exp(scores) * keep
            probs = (weights / jnp.sum(weights, axis=-1, keepdims=True)).astype(BF)
            attn[group, s, :, cols] = jnp.dot(probs, value, preferred_element_type=F32).astype(BF)

    def project(group):
        for n in range(4):
            cols = slice(n * 512, (n + 1) * 512)
            total = jnp.dot(attn[group, 0], w_out[0, :, cols], preferred_element_type=F32)
            total = total + jnp.dot(attn[group, 1], w_out[1, :, cols], preferred_element_type=F32)
            branch_send[group, :, cols] = total.astype(BF)
    def branch_copy(group, half):
        rows = pl.ds(half * 128, 128)
        src, dst = branch_send.at[group, rows, :], branch_recv.at[x, rows, :]
        for index in range(4):
            sem_id("branch", half, index)
        slot = sem_id("branch", half, 0) + x
        return src, dst, slot, pltpu.make_async_remote_copy(
            src_ref=src, dst_ref=dst, send_sem=send_sem.at[sem_id("bs", group, half)],
            recv_sem=recv_sem.at[slot],
            device_id={"grp": grp, "tp": (2 * c + group) * 2 + zhi}, device_id_type=MESH,
        )

    def branch_start(group, half):
        src, dst, slot, copy = branch_copy(group, half)

        @pl.when(x == 2 * c + group)
        def _():
            pltpu.make_async_copy(src, dst, recv_sem.at[slot]).start()

        @pl.when(x != 2 * c + group)
        def _():
            copy.start()

    def branch_sent(group, half):
        copy = branch_copy(group, half)[3]

        @pl.when(x != 2 * c + group)
        def _():
            copy.wait_send()

    def ready(copies):
        for copy in copies:
            copy.wait()

    ready(load_z)
    for group in range(2):
        remote(z_source.at[group], slab(group, tp), ("z", group), dev(dz=4)).start()
    ready(load_own)
    spread(0, tp)
    remote(parents.at[3], table.at[0], ("halo", 1), grp_at(1)).start()
    remote(parents.at[0], table.at[5], ("halo", -1), grp_at(-1)).start()
    ready(load_cross)
    chain_start(CROSS)
    ready(load_cout)
    chain_start(COUT)
    ready(load_query)
    chain_start(KEYS)
    ready(load_out)
    chain_start(VALUES)
    chain_start(OUT)
    choose()
    spread_relay(0)
    chain_relay(CROSS)
    chain_relay(COUT)
    chain_relay(KEYS)
    chain_relay(VALUES)
    for group in range(2):
        arrived(slab(group, tp_at(0, 1)), ("z", group))
    spread(1, tp_at(0, 1))
    chain_relay(OUT)
    fold_slice(0, zhi)
    fold_start(0)
    y_middle(CROSS)
    y_middle(COUT)
    spread_relay(1)
    y_middle(KEYS)
    y_end(CROSS)
    y_end(COUT)
    fold_slice(1, other)
    fold_start(1)
    spread_end(0)
    spread_end(1)
    normalise(0)
    y_middle(VALUES)
    normalise(1)
    attend(0, zhi)
    y_middle(OUT)
    attend(1, zhi)
    y_end(KEYS)
    y_end(VALUES)
    attend(0, other)
    y_end(OUT)
    project(0)
    branch_start(0, 0)
    attend(1, other)
    project(1)
    branch_start(1, 0)
    branch_sent(0, 0)
    branch_start(0, 1)
    branch_sent(1, 0)
    branch_start(1, 1)
    blocks[...] = (
        lax.div(lax.broadcasted_iota(jnp.int32, (512, 512), 0), 32)
        == lax.div(lax.broadcasted_iota(jnp.int32, (512, 512), 1), 32)
    ).astype(F32).astype(BF)

    def final_copy(i):
        near, far = lax.div(i, 8), lax.rem(i, 8)
        target = group_at(zhi, own_group) * 8 + near
        src = result.at[pl.ds(pl.multiple_of(near * 32, 32), 32), columns(far)]
        dst = out.at[grp]
        return target, far, src, dst, pltpu.make_async_remote_copy(
            src_ref=src, dst_ref=dst, send_sem=final_sem.at[i], recv_sem=out_sem,
            device_id={"grp": target, "tp": far}, device_id_type=MESH,
        )

    @pl.when(owner)
    def _():
        mod = rows_all[own_group, ROWS:EXT, :].astype(F32)
        gate1, shift2, scale2, gate2 = mod[2:3], mod[3:4], mod[4:5], mod[5:6]
        for half in range(2):
            for index in range(4):
                arrived(
                    branch_recv.at[index, pl.ds(half * 128, 128), :], ("branch", half, 0), index
                )

            @pl.loop(0, 4)
            def _(i):
                rows = pl.ds(pl.multiple_of(half * 128 + i * 32, 32), 32)
                total = branch_recv[0, rows, :].astype(F32)
                for index in range(1, 4):
                    total = total + branch_recv[index, rows, :].astype(F32)
                value = (rows_all[own_group, rows, :].astype(F32) + gate1 * total).astype(BF)
                x_one[rows, :] = value
                hidden[0, rows, :] = norm_rows(value.astype(F32), scale2, shift2).astype(BF)

            for phase in range(2 if half == 0 else 0):
                index = zhi if phase == 0 else other
                for source in range(4):
                    rows = pl.ds(pl.multiple_of(source * 128 + index * 64, 64), 64)
                    for side in range(2):
                        arrived(fold.at[side, rows, :], ("fold", phase, 0), source * 2 + side)

            rows = pl.ds(half * 128, 128)
            scores = lax.dot_general(
                hidden[0, rows, :], fold[0], (((1,), (1,)), ((), ())), preferred_element_type=F32
            )
            weights = jnp.exp(scores).astype(BF)
            total = jnp.dot(weights, blocks[...], preferred_element_type=F32)
            probs = (weights.astype(F32) / total).astype(BF)
            for n in range(4):
                cols = slice(n * 512, (n + 1) * 512)
                branch = jnp.dot(probs, fold[1, :, cols], preferred_element_type=F32)
                result[rows, cols] = (
                    x_one[rows, cols].astype(F32) + gate2[:, cols] * branch
                ).astype(BF)

            @pl.loop(half * 32, half * 32 + 32)
            def _(j):
                target, far, src, dst, copy = final_copy(j)
                mine = jnp.logical_and(target == grp, far == tp)

                @pl.when(mine)
                def _():
                    pltpu.make_async_copy(src, dst, out_sem).start()

                @pl.when(jnp.logical_not(mine))
                def _():
                    copy.start()

    for copy in sends:
        copy.wait_send()
    for condition, copy in guarded:

        @pl.when(condition)
        def _():
            copy.wait_send()

    branch_sent(0, 1)
    branch_sent(1, 1)

    @pl.when(owner)
    def _():
        @pl.loop(0, 64)
        def _(j):
            target, far, src, dst, copy = final_copy(j)

            @pl.when(jnp.logical_or(target != grp, far != tp))
            def _():
                copy.wait_send()

    pltpu.make_async_remote_copy(
        src_ref=out, dst_ref=out, send_sem=send_sem.at[0], recv_sem=out_sem,
        device_id=dev(dc=1), device_id_type=MESH,
    ).wait_recv()
    assert len(names) <= 192 and locals_used[0] <= 32


def on_device(
    latents, parents, parent_pairs, timestep, valid_frames, w_mod, w_qkv, w_out, w_cq, w_ckv, w_cout
):
    groups = parent_pairs.shape[0]
    temb = embed_time(timestep)
    mod = jnp.einsum("gt,tkd->gkd", temb, w_mod, preferred_element_type=F32).astype(BF)
    valid = jnp.broadcast_to(valid_frames.astype(BF)[:, None, None], (groups, 1, 256))
    modx = jnp.concatenate([mod, valid, jnp.zeros((groups, 9, 256), BF)], axis=1)
    wqkv = w_qkv.transpose(1, 2, 0, 3).reshape(6, D, HD)
    wckv = w_ckv.transpose(1, 2, 0, 3).reshape(4, D, HD)
    wcq = w_cq.transpose(1, 0, 2)
    hbm = pl.BlockSpec(memory_space=pl.ANY)
    moved = pl.pallas_call(
        kernel,
        out_shape=jax.ShapeDtypeStruct((32, 32, 256), BF),
        in_specs=[hbm] * 8 + [pl.BlockSpec(memory_space=pltpu.SMEM)],
        out_specs=hbm,
        scratch_shapes=[
            pltpu.VMEM((2, EXT, D), BF),
            pltpu.VMEM((2, EXT, 256), BF),
            pltpu.VMEM((2, D, 768), BF),
            pltpu.VMEM((2, D, 256), BF),
            pltpu.VMEM((2, 2 * HD, D), BF),
            pltpu.VMEM((2, 2 * HD, D), BF),
            pltpu.VMEM((D, 512), BF),
            pltpu.VMEM((6, P_SIZE, D), BF),
            pltpu.VMEM((128, D), BF),
            pltpu.VMEM((128, 512), BF),
            pltpu.VMEM((64, 512), BF),
            pltpu.VMEM((2, ROWS, D), BF),
            pltpu.VMEM((ROWS, 768), BF),
            pltpu.VMEM((2, 2, ROWS, 2 * HD), BF),
            pltpu.VMEM((2, ROWS, D), BF),
            pltpu.VMEM((4, ROWS, D), BF),
            pltpu.VMEM((2, 2, 2, 64, D), BF),
            pltpu.VMEM((2, 512, D), BF),
            pltpu.VMEM((ROWS, D), BF),
            pltpu.VMEM((ROWS, D), BF),
            pltpu.VMEM((512, 512), BF),
            pltpu.SemaphoreType.DMA((32,)),
            pltpu.SemaphoreType.DMA((192,)),
            pltpu.SemaphoreType.DMA((192,)),
            pltpu.SemaphoreType.DMA((64,)),
            pltpu.SemaphoreType.DMA,
        ],
        compiler_params=pltpu.CompilerParams(
            collective_id=0, has_side_effects=True, vmem_limit_bytes=58 << 20
        ),
        name="dit_block",
    )(
        latents.reshape(groups, ROWS, 256), modx, parents, wqkv, wckv, wcq,
        w_out.reshape(2 * HD, D), w_cout.reshape(2 * HD, D), parent_pairs,
    )
    return moved.reshape(32, 2, P_SIZE, 256)


def solution(mesh):
    in_specs = (
        P("grp", "tp"),
        P("grp", None, None),
        P("grp", None),
        P("grp"),
        P("grp"),
        P(None, None, "tp"),
        P(None, None, "tp", None),
        P("tp", None, None),
        P(None, "tp", None),
        P(None, None, "tp", None),
        P("tp", None, None),
    )
    out_specs = P(None, "grp", None, "tp")
    return jax.shard_map(
        on_device, mesh=mesh, in_specs=in_specs, out_specs=out_specs, check_vma=False
    )
```
